256 devices in a mesh: row: 64 (over x, y_hi, z), chan: 4 (over y_lo, core).
Axes of the slice: x: 4, y: 4 (y_hi: 2, y_lo: 2; y = y_hi * 2 + y_lo), z: 8, core: 2. Of those that a mesh axis runs over, the one named last changes fastest.
Arguments:
- image: bfloat16 [32, 4096, 4096], P('chan', 'row'), may hold values from -6 to 6
- spec_weight: bfloat16 [2, 256, 32, 32, 256], P(None, 'row', None, 'chan'), may hold values from -0.75 to 0.75
- point_weight: bfloat16 [32, 32], replicated, may hold values from -1 to 1
- bias: float32 [32], P('chan'), may hold values from -3 to 3
Outputs:
- layer_out: bfloat16 [32, 4096, 4096], P('chan', 'row')
The draws below stay inside these ranges and needn't reach their ends.
All inputs are finite; a program needn't handle non-finite values.
Results may differ from the reference program's by a relative error of at most 0.012.
Values may be sent and summed in bfloat16 or wider, within the bound.
No kernel may reach another device: no remote copies, remote signals or barrier semaphores. Data moves between devices by JAX's collectives and lax.ppermute only.
A program may use at most 128 MiB of HBM per device.

```python
import math
import jax
import jax.numpy as jnp
from jax import lax

C = 32
H = 4096
W = 4096
MX = 256
MY = 256


def levels(key, shape, pieces, least, largest):
    factor_of = 1.0
    for dim, parts in pieces:
        steps = jax.random.uniform(jax.random.fold_in(jax.random.fold_in(key, 6), dim), (parts,), jnp.float32, least / len(pieces), largest / len(pieces))
        factor_of = factor_of * jnp.repeat(jnp.exp(steps), shape[dim] // parts).reshape((-1,) + (1,) * (len(shape) - 1 - dim))
    return factor_of


def centred(rng, shape, spread, bound, split=(), kind=jnp.bfloat16):
    level = levels(rng, shape, split, -0.22, 0.18) if split else 1.0
    result = jax.random.normal(rng, shape, jnp.float32) * spread * level
    return jnp.minimum(jnp.maximum(result, -bound), bound).astype(kind)


def setup_inputs(seed: int = 0) -> dict:
    streams_of = jax.random.split(jax.random.key(seed), 5)
    image = centred(streams_of[0], (C, H, W), 1.0, 6.0, ((0, 4), (1, 64)))
    spec_weight = centred(streams_of[1], (2, MX, C, C, MY), (2 * C) ** -0.5, 0.75, ((1, 64), (3, 4)))
    point_weight = centred(streams_of[2], (C, C), C ** -0.5, 1.0)
    bias = centred(streams_of[3], (C,), 0.5, 3.0, ((0, 4),), jnp.float32)
    return {"image": image, "spec_weight": spec_weight, "point_weight": point_weight, "bias": bias}


def wave_table(points, freqs, length):
    prod = jnp.mod(points[:, None] * freqs[None, :], length)
    angle = prod.astype(jnp.float32) * (2.0 * math.pi / length)
    return (jnp.cos(angle), jnp.sin(angle))

def reference(image, spec_weight, point_weight, bias):
    col_pts = jnp.arange(W, dtype=jnp.int32)
    col_freq = jnp.arange(MY, dtype=jnp.int32)
    cos_w, sin_w = wave_table(col_pts, col_freq, W)
    fwd_cols = jnp.concatenate([cos_w, -sin_w], 1).astype(jnp.bfloat16)
    back_cols = jnp.concatenate([cos_w.T, -sin_w.T], 0).astype(jnp.bfloat16)
    row_pts = jnp.arange(H, dtype=jnp.int32)
    row_freq = jnp.arange(MX, dtype=jnp.int32) - MX // 2
    cos_h, sin_h = wave_table(row_pts, row_freq, H)
    fwd_rows = jnp.concatenate([cos_h, sin_h], 1).T.astype(jnp.bfloat16)

    def forward(plane):
        colspec = (jnp.dot(plane, fwd_cols, preferred_element_type=jnp.float32) * (1.0 / math.sqrt(W))).astype(jnp.bfloat16)
        partial_value = jnp.dot(fwd_rows, colspec, preferred_element_type=jnp.float32)
        spec_re = partial_value[:MX, :MY] + partial_value[MX:, MY:]
        spec_im = partial_value[:MX, MY:] - partial_value[MX:, :MY]
        return (jnp.concatenate([spec_re, spec_im], 1) * (1.0 / math.sqrt(H))).astype(jnp.bfloat16)
    spectrum = lax.map(forward, image)
    zed_re = spectrum[..., :MY].astype(jnp.float32)
    zed_im = spectrum[..., MY:].astype(jnp.float32)
    wgt_re = spec_weight[0].astype(jnp.float32)
    wgt_im = spec_weight[1].astype(jnp.float32)
    mix_re = jnp.einsum('kiop,ikp->okp', wgt_re, zed_re) - jnp.einsum('kiop,ikp->okp', wgt_im, zed_im)
    mix_im = jnp.einsum('kiop,ikp->okp', wgt_re, zed_im) + jnp.einsum('kiop,ikp->okp', wgt_im, zed_re)
    mixed = jnp.concatenate([mix_re, mix_im], -1).astype(jnp.bfloat16).astype(jnp.float32)
    cos_back = cos_h.T.astype(jnp.bfloat16).astype(jnp.float32)
    sin_back = sin_h.T.astype(jnp.bfloat16).astype(jnp.float32)
    with_cos = jnp.einsum('okp,kh->ohp', mixed, cos_back)
    with_sin = jnp.einsum('okp,kh->ohp', mixed, sin_back)
    back_re = with_cos[..., :MY] - with_sin[..., MY:]
    back_im = with_sin[..., :MY] + with_cos[..., MY:]
    rowback = (jnp.concatenate([back_re, back_im], -1) * (1.0 / math.sqrt(MX))).astype(jnp.bfloat16)
    flat_image = image.reshape(C, H * W)

    def out_channel(channel):
        spectral = jnp.dot(rowback[channel], back_cols, preferred_element_type=jnp.float32) * (1.0 / math.sqrt(MY))
        weight_row = lax.dynamic_slice_in_dim(point_weight, channel, 1, 0)
        pointwise = jnp.dot(weight_row, flat_image, preferred_element_type=jnp.float32).reshape(H, W).astype(jnp.bfloat16)
        total = spectral + pointwise.astype(jnp.float32) + bias[channel]
        return jax.nn.gelu(total, approximate=False).astype(jnp.bfloat16)
    return lax.map(out_channel, jnp.arange(C, dtype=jnp.int32))
```

```python
import math

import jax
import jax.numpy as jnp
import ml_dtypes
import numpy as np
from jax import lax
from jax.sharding import Mesh, PartitionSpec as P

H = 4096
W = 4096
MX = 256
MY = 256
PAIR = [(0, 1), (1, 0)]
CHUNKS = 4


def wave_table(points, freqs, length):
    prod = np.mod(points[:, None] * freqs[None, :], length)
    one = np.arange(length).astype(np.float32) * np.float32(2.0 * math.pi / length)
    return np.cos(one)[prod], np.sin(one)[prod]


def tables():
    cos_w, sin_w = wave_table(np.arange(W), np.arange(MY), W)
    cols = np.concatenate([cos_w, -sin_w], 1)
    cos_h, sin_h = wave_table(np.arange(H), np.arange(MX) - MX // 2, H)
    rows = np.concatenate([cos_h, sin_h], 1)
    return cols.astype(ml_dtypes.bfloat16), rows.astype(ml_dtypes.bfloat16)


def on_device(image, spec_weight, point_weight, bias):
    chan, rows, width = image.shape
    cols_np, rows_np = tables()
    fwd_cols = jnp.asarray(cols_np)
    back_cols = jnp.asarray(np.ascontiguousarray(cols_np.T))
    row_group = lax.axis_index(("x", "yh")) * (8 * rows)
    row_tab = lax.dynamic_slice_in_dim(jnp.asarray(rows_np), row_group, 8 * rows, 0)

    step = rows // CHUNKS
    sibling = lax.ppermute(image, "core", PAIR)
    cross = [lax.ppermute(image[:, j * step : (j + 1) * step], "yl", PAIR) for j in range(CHUNKS)]
    cross_sib = [lax.ppermute(c, "core", PAIR) for c in cross]

    with jax.named_scope("colspec"):
        colspec = jnp.dot(
            image.reshape(chan * rows, width), fwd_cols, preferred_element_type=jnp.float32
        )
        colspec = (colspec * (1.0 / math.sqrt(W))).astype(jnp.bfloat16)
    with jax.named_scope("swap_rows"):
        line = lax.all_to_all(colspec.reshape(chan, rows, 2 * MY), "z", 0, 0, tiled=True)
    line = line.reshape(8 * rows, 2 * MY)
    with jax.named_scope("row_dft"):
        part = lax.dot_general(
            row_tab, line, (((0,), (0,)), ((), ())), preferred_element_type=jnp.float32
        )
        spec_re = part[:MX, :MY] + part[MX:, MY:]
        spec_im = part[:MX, MY:] - part[MX:, :MY]
        part = jnp.concatenate([spec_re, spec_im], -1) * (1.0 / math.sqrt(H))
        part = part.astype(jnp.bfloat16).reshape(64, MX // 64, 2 * MY)
    with jax.named_scope("swap_modes"):
        part = lax.all_to_all(part, ("x", "yh", "z"), 0, 0, tiled=True)
    with jax.named_scope("sum_lines"):
        spectrum = jnp.sum(
            part.reshape(8, 8, MX // 64, 2 * MY).astype(jnp.float32), 0
        ).astype(jnp.bfloat16)
    with jax.named_scope("gather_chan"):
        zed = lax.all_gather(spectrum, ("yl", "core"), axis=0, tiled=True)
    with jax.named_scope("mix"):
        zed_re = zed[..., :MY].astype(jnp.float32)
        zed_im = zed[..., MY:].astype(jnp.float32)
        wgt_re = spec_weight[0].astype(jnp.float32)
        wgt_im = spec_weight[1].astype(jnp.float32)
        mix_re = jnp.einsum("kiop,ikp->okp", wgt_re, zed_re) - jnp.einsum(
            "kiop,ikp->okp", wgt_im, zed_im
        )
        mix_im = jnp.einsum("kiop,ikp->okp", wgt_re, zed_im) + jnp.einsum(
            "kiop,ikp->okp", wgt_im, zed_re
        )
        mixed = jnp.concatenate([mix_re, mix_im], -1).astype(jnp.bfloat16)
        mixed = jnp.broadcast_to(mixed[None], (8,) + mixed.shape).reshape(64, MX // 64, 2 * MY)
    with jax.named_scope("spread_modes"):
        modes = lax.all_to_all(mixed, ("x", "yh", "z"), 0, 0, tiled=True).reshape(MX, 2 * MY)
    with jax.named_scope("rowback"):
        mode_re, mode_im = modes[:, :MY], modes[:, MY:]
        turned = jnp.concatenate(
            [modes, jnp.concatenate([-mode_im, mode_re], 1)], 0
        )
        back = jnp.dot(row_tab, turned, preferred_element_type=jnp.float32)
        back = (back * (1.0 / math.sqrt(MX))).astype(jnp.bfloat16).reshape(8, rows, 2 * MY)
    with jax.named_scope("swap_back"):
        back = lax.all_to_all(back, "z", 0, 0, tiled=True)
    with jax.named_scope("final"):
        spectral = jnp.dot(
            back.reshape(chan * rows, 2 * MY), back_cols, preferred_element_type=jnp.float32
        )
        spectral = (spectral * (1.0 / math.sqrt(MY))).reshape(chan, rows, width)
        me = lax.axis_index(("yl", "core"))
        mine = lax.dynamic_slice(point_weight, (me * chan, 0), (chan, 4 * chan))
        blocks = [
            lax.dynamic_slice(mine, (0, (me ^ s) * chan), (chan, chan)) for s in range(4)
        ]
        order = jnp.concatenate(blocks, 1)
        feats = jnp.concatenate(
            [image, sibling, jnp.concatenate(cross, 1), jnp.concatenate(cross_sib, 1)], 0
        )
        pointwise = jnp.einsum(
            "oi,ihw->ohw", order, feats, preferred_element_type=jnp.float32
        ).astype(jnp.bfloat16)
        total = spectral + pointwise.astype(jnp.float32) + bias[:, None, None]
        return jax.nn.gelu(total, approximate=False).astype(jnp.bfloat16)


def solution(mesh):
    fine = Mesh(mesh.devices.reshape(4, 2, 8, 2, 2), ("x", "yh", "z", "yl", "core"))
    row, chan = ("x", "yh", "z"), ("yl", "core")
    in_specs = (P(chan, row, None), P(None, row, None, chan, None), P(), P(chan))
    return jax.shard_map(
        on_device, mesh=fine, in_specs=in_specs, out_specs=P(chan, row, None), check_vma=False
    )
```

```python
import functools
import math

import jax
import jax.numpy as jnp
import ml_dtypes
import numpy as np
from jax import lax
from jax.experimental import pallas as pl
from jax.experimental.pallas import tpu as pltpu
from jax.sharding import Mesh, PartitionSpec as P

H = 4096
W = 4096
MX = 256
MY = 256
PAIR = [(0, 1), (1, 0)]
GROUP = 16
VMEM = 56 * 2**20
TILE = 512
CUTS = (0, 1024, 2048, 3072, 4096)
RAW = 2


def wave_table(points, freqs, length):
    prod = np.mod(points[:, None] * freqs[None, :], length)
    one = np.arange(length).astype(np.float32) * np.float32(2.0 * math.pi / length)
    return np.cos(one)[prod], np.sin(one)[prod]


def tables():
    cos_w, sin_w = wave_table(np.arange(W), np.arange(MY), W)
    cols = np.concatenate([cos_w, -sin_w], 1)
    freq = np.arange(MX).reshape(4, 2, 8, 4).transpose(0, 2, 1, 3).reshape(-1) - MX // 2
    cos_h, sin_h = wave_table(np.arange(H), freq, H)
    rows = np.concatenate([cos_h, sin_h], 1).reshape(4, 8, 2 * 64, 2 * MX)
    return cols.astype(ml_dtypes.bfloat16), rows.astype(ml_dtypes.bfloat16)


def spread(point_weight, outputs, inputs, chan):
    mine = lax.dynamic_slice(point_weight, (outputs * chan, 0), (chan, 4 * chan))
    order = jnp.concatenate(
        [lax.dynamic_slice(mine, (0, i * chan), (chan, chan)) for i in inputs], 1
    )
    n = len(inputs) * chan
    tall = np.kron(np.eye(chan), np.ones((GROUP, 1)))
    wide = np.kron(np.eye(n), np.ones((1, GROUP)))
    same = np.tile(np.eye(GROUP), (chan, n))
    full = jnp.dot(jnp.asarray(tall, jnp.bfloat16), order)
    full = jnp.dot(full, jnp.asarray(wide, jnp.bfloat16))
    return full * jnp.asarray(same, jnp.bfloat16)


def product_kernel(own_ref, sib_ref, kron_ref, out_ref):
    for g in range(own_ref.shape[1] // GROUP):
        at = pl.ds(g * GROUP, GROUP)
        feats = jnp.concatenate(
            [r[:, at, :].reshape(8 * GROUP, TILE) for r in (own_ref, sib_ref)], 0
        )
        total = jnp.dot(kron_ref[...], feats, preferred_element_type=jnp.float32)
        out_ref[:, at, :] = total.astype(jnp.bfloat16).reshape(8, GROUP, TILE)


def product(begin, end, image, sibling, kron):
    chan, rows, _ = image.shape
    first, steps = begin // TILE, (end - begin) // TILE
    whole = pl.BlockSpec((chan, rows, TILE), lambda w: (0, 0, first + w))
    return pl.pallas_call(
        product_kernel,
        grid=(steps,),
        in_specs=[whole, whole, pl.BlockSpec(kron.shape, lambda w: (0, 0))],
        out_specs=pl.BlockSpec((chan, rows, TILE), lambda w: (0, 0, w)),
        out_shape=jax.ShapeDtypeStruct((chan, rows, end - begin), jnp.bfloat16),
        compiler_params=pltpu.CompilerParams(vmem_limit_bytes=VMEM),
        cost_estimate=pl.CostEstimate(
            flops=2 * 8 * rows * TILE * 256 * steps,
            bytes_accessed=3 * 2**19 * steps,
            transcendentals=0,
        ),
        name="product",
    )(image, sibling, kron)


def last_kernel(ends, raw, *refs):
    rb_ref, back_ref, own_ref, sib_ref, kron_ref, bias_ref = refs[:6]
    cross_refs, out_ref = refs[6:], refs[-1]
    rows = rb_ref.shape[1]

    def one(cross, is_raw):
        for g in range(rows // GROUP):
            at = pl.ds(g * GROUP, GROUP)
            feats = (own_ref, sib_ref, *cross) if is_raw else (own_ref, sib_ref)
            feats = jnp.concatenate([r[:, at, :].reshape(8 * GROUP, TILE) for r in feats], 0)
            total = jnp.dot(
                rb_ref[:, at, :].reshape(8 * GROUP, 2 * MY),
                back_ref[...],
                preferred_element_type=jnp.float32,
            )
            total += jnp.dot(
                kron_ref[:, : feats.shape[0]], feats, preferred_element_type=jnp.float32
            )
            total += bias_ref[...]
            if not is_raw:
                total += cross[0][:, at, :].reshape(8 * GROUP, TILE).astype(jnp.float32)
            out = 0.5 * total * (1.0 + lax.erf(total * math.sqrt(0.5)))
            out_ref[:, at, :] = out.astype(jnp.bfloat16).reshape(8, GROUP, TILE)

    w = pl.program_id(0)
    at = 0
    for p, is_raw in enumerate(raw):
        n = 2 if is_raw else 1
        cross = cross_refs[at : at + n]
        at += n
        if len(raw) == 1:
            one(cross, is_raw)
            return

        @pl.when((w >= (ends[p - 1] if p else 0)) & (w < ends[p]))
        def _(cross=cross, is_raw=is_raw):
            one(cross, is_raw)


def last(begin, rb, back_cols, image, sibling, cross, kron, bias_rows, so_far):
    chan, rows, width = image.shape
    first = begin // TILE
    ends = tuple(np.cumsum([c[0].shape[2] // TILE for c in cross]).tolist())
    raw = tuple(len(c) == 2 for c in cross)
    whole = pl.BlockSpec((chan, rows, TILE), lambda w: (0, 0, first + w))
    in_specs = [
        pl.BlockSpec((chan, rows, 2 * MY), lambda w: (0, 0, 0)),
        pl.BlockSpec((2 * MY, TILE), lambda w: (0, first + w)),
        whole,
        whole,
        pl.BlockSpec(kron.shape, lambda w: (0, 0)),
        pl.BlockSpec(bias_rows.shape, lambda w: (0, 0)),
    ]
    args = [rb, back_cols, image, sibling, kron, bias_rows]
    for p, c in enumerate(cross):
        lo, hi = (ends[p - 1] if p else 0), ends[p]
        for array in c:
            args.append(array)
            in_specs.append(
                pl.BlockSpec(
                    (chan, rows, TILE),
                    lambda w, lo=lo, hi=hi: (0, 0, jnp.clip(w - lo, 0, hi - lo - 1)),
                )
            )
    alias = {}
    if so_far is not None:
        in_specs.append(pl.BlockSpec(memory_space=pl.ANY))
        alias = {len(args): 0}
        args.append(so_far)
    return pl.pallas_call(
        functools.partial(last_kernel, ends, raw),
        grid=(ends[-1],),
        in_specs=in_specs,
        out_specs=whole,
        out_shape=jax.ShapeDtypeStruct((chan, rows, width), jnp.bfloat16),
        input_output_aliases=alias,
        compiler_params=pltpu.CompilerParams(vmem_limit_bytes=VMEM),
        cost_estimate=pl.CostEstimate(
            flops=4 * 8 * rows * TILE * 512 * ends[-1],
            bytes_accessed=3 * 2**20 * ends[-1],
            transcendentals=0,
        ),
        name="last",
    )(*args)


def on_device(image, spec_weight, point_weight, bias):
    chan, rows, width = image.shape
    cols_np, rows_np = tables()
    fwd_cols = jnp.asarray(cols_np)
    back_cols = jnp.asarray(np.ascontiguousarray(cols_np.T))
    row_at = lax.axis_index(("yh", "zh"))
    row_tab = lax.dynamic_slice_in_dim(jnp.asarray(rows_np), row_at, 1, 1).reshape(
        8 * rows, 2 * MX
    )
    group, column = ("x", "zl"), ("x", "zh", "zl")

    def cut(src, j):
        return src[:, :, CUTS[j] : CUTS[j + 1]]

    def send(src):
        return lax.ppermute(src, "yl", PAIR)

    parts = len(CUTS) - 1
    cross = [send(cut(image, 0))]
    sibling = lax.ppermute(image, "core", PAIR)
    with jax.named_scope("point_weights"):
        me = lax.axis_index(("yl", "core"))
        kron = spread(point_weight, me, [me, me ^ 1, me ^ 2, me ^ 3], chan)
        kron_other = spread(point_weight, me ^ 2, [me, me ^ 1], chan)
        bias_rows = jnp.repeat(bias, GROUP)[:, None]

    with jax.named_scope("colspec"):
        colspec = jnp.dot(
            image.reshape(chan * rows, width), fwd_cols, preferred_element_type=jnp.float32
        )
        colspec = (colspec * (1.0 / math.sqrt(W))).astype(jnp.bfloat16)
    later, colspec = lax.optimization_barrier((image, colspec))
    cross += [send(cut(later, j)) for j in range(1, RAW)]
    with jax.named_scope("swap_rows"):
        line = lax.all_to_all(colspec.reshape(chan, rows, 2 * MY), group, 0, 0, tiled=True)
    line = line.reshape(8 * rows, 2 * MY)
    line, cross[0] = lax.optimization_barrier((line, cross[0]))
    with jax.named_scope("row_dft"):
        part = lax.dot_general(
            row_tab, line, (((0,), (0,)), ((), ())), preferred_element_type=jnp.float32
        )
        spec_re = part[:MX, :MY] + part[MX:, MY:]
        spec_im = part[:MX, MY:] - part[MX:, :MY]
        part = jnp.concatenate([spec_re, spec_im], -1) * (1.0 / math.sqrt(H))
        part = part.astype(jnp.bfloat16).reshape(32, 8, 2 * MY)
    with jax.named_scope("swap_modes"):
        part = lax.all_to_all(part, column, 0, 0, tiled=True)
    with jax.named_scope("products"):
        made = [
            product(CUTS[j], CUTS[j + 1], image, sibling, kron_other) for j in range(RAW, parts)
        ]
    part, kron, *made = lax.optimization_barrier((part, kron, *made))
    with jax.named_scope("sum_lines"):
        part = jnp.sum(part.reshape(4, 4, 2, 8, 2 * MY).astype(jnp.float32), 1)
        part = part.astype(jnp.bfloat16).reshape(8, 2, 4, 2 * MY).transpose(1, 0, 2, 3)
        part = jnp.broadcast_to(part[:, None], (2, 4, 8, 4, 2 * MY)).reshape(64, 4, 2 * MY)
    with jax.named_scope("gather_chan"):
        part = lax.all_to_all(part, ("yh", "yl", "core"), 0, 0, tiled=True)
        part, cross[1] = lax.optimization_barrier((part, cross[1]))
        zed = jnp.sum(part.reshape(2, 32, 4, 2 * MY).astype(jnp.float32), 0).astype(jnp.bfloat16)
    with jax.named_scope("mix"):
        zed_re = zed[..., :MY].astype(jnp.float32)
        zed_im = zed[..., MY:].astype(jnp.float32)
        wgt_re = spec_weight[0].astype(jnp.float32)
        wgt_im = spec_weight[1].astype(jnp.float32)
        mix_re = jnp.einsum("kiop,ikp->okp", wgt_re, zed_re) - jnp.einsum(
            "kiop,ikp->okp", wgt_im, zed_im
        )
        mix_im = jnp.einsum("kiop,ikp->okp", wgt_re, zed_im) + jnp.einsum(
            "kiop,ikp->okp", wgt_im, zed_re
        )
        mixed = jnp.concatenate([mix_re, mix_im], -1).astype(jnp.bfloat16)
    with jax.named_scope("join_halves"):
        other = lax.ppermute(mixed, "yh", PAIR)
        other, *made = lax.optimization_barrier((other, *made))
        cross += [send(c) for c in made]
        first = lax.axis_index("yh") == 0
        mixed = jnp.concatenate(
            [jnp.where(first, mixed, other), jnp.where(first, other, mixed)], 1
        )
        mixed = mixed.reshape(4, 1, 2, 8, 2 * MY)
        mixed = jnp.broadcast_to(mixed, (4, 4, 2, 8, 2 * MY)).reshape(32, 8, 2 * MY)
    with jax.named_scope("spread_modes"):
        modes = lax.all_to_all(mixed, column, 0, 0, tiled=True).reshape(MX, 2 * MY)
    modes, cross[RAW] = lax.optimization_barrier((modes, cross[RAW]))
    with jax.named_scope("rowback"):
        mode_re, mode_im = modes[:, :MY], modes[:, MY:]
        turned = jnp.concatenate([modes, jnp.concatenate([-mode_im, mode_re], 1)], 0)
        back = jnp.dot(row_tab, turned, preferred_element_type=jnp.float32)
        back = (back * (1.0 / math.sqrt(MX) / math.sqrt(MY))).astype(jnp.bfloat16)
        back = back.reshape(8, rows, 2 * MY)
    with jax.named_scope("swap_back"):
        back = lax.all_to_all(back, group, 0, 0, tiled=True)
    cross = [(c, lax.ppermute(c, "core", PAIR)) if j < RAW else (c,) for j, c in enumerate(cross)]
    out = None
    for lo, hi in ((0, parts - 1), (parts - 1, parts)):
        out = last(
            CUTS[lo], back, back_cols, image, sibling, cross[lo:hi], kron, bias_rows, out
        )
    return out


def solution(mesh):
    fine = Mesh(mesh.devices.reshape(4, 2, 4, 2, 2, 2), ("x", "yh", "zh", "zl", "yl", "core"))
    row, chan = ("x", "yh", "zh", "zl"), ("yl", "core")
    in_specs = (P(chan, row, None), P(None, row, None, chan, None), P(), P(chan))
    return jax.shard_map(
        on_device, mesh=fine, in_specs=in_specs, out_specs=P(chan, row, None), check_vma=False
    )
```

```python
import functools
import math

import jax
import jax.numpy as jnp
import ml_dtypes
import numpy as np
from jax import lax
from jax.experimental import pallas as pl
from jax.experimental.pallas import tpu as pltpu
from jax.sharding import Mesh, PartitionSpec as P

H = 4096
W = 4096
MX = 256
MY = 256
PAIR = [(0, 1), (1, 0)]
GROUP = 16
VMEM = 56 * 2**20
SMALL = 16 * 2**20
TILE = 512
RAW = 2048
RAW_CUTS = (0, 1024, RAW)


def wave_table(points, freqs, length):
    prod = np.mod(points[:, None] * freqs[None, :], length)
    one = np.arange(length).astype(np.float32) * np.float32(2.0 * math.pi / length)
    return np.cos(one)[prod], np.sin(one)[prod]


def tables():
    cos_w, sin_w = wave_table(np.arange(W), np.arange(MY), W)
    cols = np.concatenate([cos_w, -sin_w], 1)
    freq = np.arange(MX).reshape(4, 2, 8, 4).transpose(0, 2, 1, 3).reshape(-1) - MX // 2
    cos_h, sin_h = wave_table(np.arange(H), freq, H)
    rows = np.concatenate([cos_h, sin_h], 1).reshape(4, 8, 2 * 64, 2 * MX)
    return cols.astype(ml_dtypes.bfloat16), rows.astype(ml_dtypes.bfloat16)


def spread(point_weight, outputs, inputs, chan):
    mine = lax.dynamic_slice(point_weight, (outputs * chan, 0), (chan, 4 * chan))
    order = jnp.concatenate(
        [lax.dynamic_slice(mine, (0, i * chan), (chan, chan)) for i in inputs], 1
    )
    n = len(inputs) * chan
    tall = np.kron(np.eye(chan), np.ones((GROUP, 1)))
    wide = np.kron(np.eye(n), np.ones((1, GROUP)))
    same = np.tile(np.eye(GROUP), (chan, n))
    full = jnp.dot(jnp.asarray(tall, jnp.bfloat16), order)
    full = jnp.dot(full, jnp.asarray(wide, jnp.bfloat16))
    return full * jnp.asarray(same, jnp.bfloat16)


def stack(refs, at):
    return jnp.concatenate([r[:, at, :].reshape(-1, TILE) for r in refs], 0)


def block(chan, rows, lo=0, hi=None):
    if hi is None:
        return pl.BlockSpec((chan, rows, TILE), lambda w: (0, 0, w + lo))
    return pl.BlockSpec(
        (chan, rows, TILE), lambda w: (0, 0, jnp.clip(w - lo, 0, hi - lo - 1))
    )


def product_kernel(
    own_ref, sib_ref, kron_ref, soon_ref, late_ref, half_ref, next_ref, end_ref
):
    step = pl.program_id(0)
    for t, (mine_ref, place, theirs) in enumerate(
        (
            (soon_ref, 0, ((next_ref, 0, 8),)),
            (late_ref, 0, ((half_ref, 0, 4), (end_ref, 0, 4))),
            (late_ref, 1, ((end_ref, 4, 8),)),
            (late_ref, 2, ((end_ref, 12, 8),)),
        )
    ):

        @pl.when(step == t)
        def _(mine_ref=mine_ref, place=place, theirs=theirs):
            for g in range(own_ref.shape[1] // GROUP):
                at = pl.ds(g * GROUP, GROUP)
                total = jnp.dot(
                    kron_ref[...],
                    stack((own_ref, sib_ref), at),
                    preferred_element_type=jnp.float32,
                )
                total = total.astype(jnp.bfloat16).reshape(16, GROUP, TILE)
                mine_ref[:, at, pl.ds(place * TILE, TILE)] = total[:8]
                done = 8
                for ref, lo, n in theirs:
                    ref[lo : lo + n, at, :] = total[done : done + n]
                    done += n


def product(image, sibling, kron):
    chan, rows, width = image.shape
    first, tiles = RAW // TILE, (width - RAW) // TILE
    sizes = [(chan, TILE), (chan, 3 * TILE), (4, TILE), (8, TILE), (20, TILE)]
    return pl.pallas_call(
        product_kernel,
        grid=(tiles,),
        in_specs=[block(chan, rows, first)] * 2 + [pl.BlockSpec(kron.shape, lambda w: (0, 0))],
        out_specs=[pl.BlockSpec((n, rows, w), lambda w: (0, 0, 0)) for n, w in sizes],
        out_shape=[jax.ShapeDtypeStruct((n, rows, w), jnp.bfloat16) for n, w in sizes],
        compiler_params=pltpu.CompilerParams(vmem_limit_bytes=VMEM),
        cost_estimate=pl.CostEstimate(
            flops=4 * 8 * rows * TILE * 256 * tiles,
            bytes_accessed=2**21 * tiles,
            transcendentals=0,
        ),
        name="product",
    )(image, sibling, kron)


def pointwise_kernel(own_ref, sib_ref, cross_ref, csib_ref, kron_ref, out_ref):
    for g in range(own_ref.shape[1] // GROUP):
        at = pl.ds(g * GROUP, GROUP)
        total = jnp.dot(
            kron_ref[...],
            stack((own_ref, sib_ref, cross_ref, csib_ref), at),
            preferred_element_type=jnp.float32,
        )
        out_ref[:, at, :] = total.astype(jnp.bfloat16).reshape(8, GROUP, TILE)


def pointwise(begin, image, sibling, cross, kron):
    chan, rows, width = cross.shape
    steps = width // TILE
    return pl.pallas_call(
        pointwise_kernel,
        grid=(steps,),
        in_specs=[block(chan, rows, begin // TILE)] * 2
        + [block(chan, rows)] * 2
        + [pl.BlockSpec(kron.shape, lambda w: (0, 0))],
        out_specs=block(chan, rows),
        out_shape=jax.ShapeDtypeStruct(cross.shape, jnp.bfloat16),
        compiler_params=pltpu.CompilerParams(vmem_limit_bytes=VMEM),
        cost_estimate=pl.CostEstimate(
            flops=2 * 8 * rows * width * 512,
            bytes_accessed=5 * 2**19 * steps,
            transcendentals=0,
        ),
        name="pointwise",
    )(image, sibling, cross, lax.ppermute(cross, "core", PAIR), kron)


def finish(rb_ref, back_ref, bias_ref, terms, out_ref, place=0):
    cols = pl.ds(place * TILE, TILE)
    for g in range(rb_ref.shape[1] // GROUP):
        at = pl.ds(g * GROUP, GROUP)
        total = jnp.dot(
            rb_ref[:, at, :].reshape(8 * GROUP, 2 * MY),
            back_ref[:, cols],
            preferred_element_type=jnp.float32,
        )
        for term in terms:
            term = [
                ref[lo : lo + n, at, pl.ds(c, TILE)].reshape(n * GROUP, TILE)
                for ref, lo, n, c in term
            ]
            total += jnp.concatenate(term, 0).astype(jnp.float32)
        total += bias_ref[...]
        out = 0.5 * total * (1.0 + lax.erf(total * math.sqrt(0.5)))
        out_ref[:, at, :] = out.astype(jnp.bfloat16).reshape(8, GROUP, TILE)


def most_kernel(rb_ref, back_ref, bias_ref, first_ref, second_ref, soon_ref, next_ref, out_ref):
    column = pl.program_id(0) * TILE

    @pl.when(column < RAW_CUTS[1])
    def _():
        finish(rb_ref, back_ref, bias_ref, ([(first_ref, 0, 8, 0)],), out_ref)

    @pl.when((column >= RAW_CUTS[1]) & (column < RAW))
    def _():
        finish(rb_ref, back_ref, bias_ref, ([(second_ref, 0, 8, 0)],), out_ref)

    @pl.when(column >= RAW)
    def _():
        terms = ([(soon_ref, 0, 8, 0)], [(next_ref, 0, 8, 0)])
        finish(rb_ref, back_ref, bias_ref, terms, out_ref)


def most(rb, back_cols, bias_rows, first, second, soon, following):
    chan, rows, _ = rb.shape
    width = back_cols.shape[1]
    cuts = [c // TILE for c in RAW_CUTS]

    def still(array):
        return pl.BlockSpec(array.shape, lambda w: (0,) * array.ndim)

    return pl.pallas_call(
        most_kernel,
        grid=(cuts[2] + 1,),
        in_specs=[
            still(rb),
            pl.BlockSpec((2 * MY, TILE), lambda w: (0, w)),
            still(bias_rows),
            block(chan, rows, 0, cuts[1]),
            block(chan, rows, cuts[1], cuts[2]),
            still(soon),
            still(following),
        ],
        out_specs=block(chan, rows),
        out_shape=jax.ShapeDtypeStruct((chan, rows, width), jnp.bfloat16),
        compiler_params=pltpu.CompilerParams(vmem_limit_bytes=VMEM),
        cost_estimate=pl.CostEstimate(flops=1, bytes_accessed=1, transcendentals=0),
        name="most",
    )(rb, back_cols, bias_rows, first, second, soon, following)


def rest_kernel(rb_ref, back_ref, bias_ref, late_ref, half_ref, end_ref, so_far_ref, out_ref):
    others = (
        [(half_ref, 0, 4, 0), (end_ref, 0, 4, 0)],
        [(end_ref, 4, 8, 0)],
        [(end_ref, 12, 8, 0)],
    )
    for t, other in enumerate(others):

        @pl.when(pl.program_id(0) == t)
        def _(t=t, other=other):
            terms = ([(late_ref, 0, 8, t * TILE)], other)
            finish(rb_ref, back_ref, bias_ref, terms, out_ref, t)


def rest(rb, back_tiles, bias_rows, late, half, end, so_far):
    chan, rows, width = so_far.shape
    whole = pl.BlockSpec(memory_space=pltpu.VMEM)
    return pl.pallas_call(
        rest_kernel,
        grid=(3,),
        in_specs=[whole] * 6 + [pl.BlockSpec(memory_space=pl.ANY)],
        out_specs=block(chan, rows, width // TILE - 3),
        out_shape=jax.ShapeDtypeStruct(so_far.shape, jnp.bfloat16),
        input_output_aliases={6: 0},
        compiler_params=pltpu.CompilerParams(vmem_limit_bytes=SMALL),
        cost_estimate=pl.CostEstimate(flops=1, bytes_accessed=1, transcendentals=0),
        name="rest",
    )(rb, back_tiles, bias_rows, late, half, end, so_far)


def on_device(image, spec_weight, point_weight, bias):
    chan, rows, width = image.shape
    cols_np, rows_np = tables()
    fwd_cols = jnp.asarray(cols_np)
    back_cols = jnp.asarray(np.ascontiguousarray(cols_np.T))
    row_at = lax.axis_index(("yh", "zh"))
    row_tab = lax.dynamic_slice_in_dim(jnp.asarray(rows_np), row_at, 1, 1).reshape(
        8 * rows, 2 * MX
    )
    group, column = ("x", "zl"), ("x", "zh", "zl")

    def send(src):
        return lax.ppermute(src, "yl", PAIR)

    def raw(src, j):
        return src[:, :, RAW_CUTS[j] : RAW_CUTS[j + 1]]

    first, later = lax.optimization_barrier((raw(image, 0), image))
    cross = [send(first)]
    sibling = lax.ppermute(later, "core", PAIR)
    with jax.named_scope("point_weights"):
        me = lax.axis_index(("yl", "core"))
        kron = spread(point_weight, me, [me, me ^ 1, me ^ 2, me ^ 3], chan)
        kron_other = spread(point_weight, me ^ 2, [me, me ^ 1], chan)
        kron_both = jnp.concatenate([kron[:, : kron.shape[1] // 2], kron_other], 0)
        bias_rows = jnp.repeat(bias, GROUP)[:, None]

    with jax.named_scope("colspec"):
        colspec = jnp.dot(
            image.reshape(chan * rows, width), fwd_cols, preferred_element_type=jnp.float32
        )
        colspec = (colspec * (1.0 / math.sqrt(W))).astype(jnp.bfloat16)
    later, _ = lax.optimization_barrier((image, colspec))
    cross += [send(raw(later, j)) for j in range(1, len(RAW_CUTS) - 1)]
    with jax.named_scope("swap_rows"):
        line = lax.all_to_all(colspec.reshape(chan, rows, 2 * MY), group, 0, 0, tiled=True)
    line = line.reshape(8 * rows, 2 * MY)
    line, cross[0] = lax.optimization_barrier((line, cross[0]))
    with jax.named_scope("row_dft"):
        part = lax.dot_general(
            row_tab, line, (((0,), (0,)), ((), ())), preferred_element_type=jnp.float32
        )
        spec_re = part[:MX, :MY] + part[MX:, MY:]
        spec_im = part[:MX, MY:] - part[MX:, :MY]
        part = jnp.concatenate([spec_re, spec_im], -1) * (1.0 / math.sqrt(H))
        part = part.astype(jnp.bfloat16).reshape(32, 8, 2 * MY)
    with jax.named_scope("swap_modes"):
        part = lax.all_to_all(part, column, 0, 0, tiled=True)
    with jax.named_scope("products"):
        soon, late, half, following, end = product(image, sibling, kron_both)
    part, kron, bias_rows, soon, late, half, following, end = lax.optimization_barrier(
        (part, kron, bias_rows, soon, late, half, following, end)
    )
    half = send(half)
    with jax.named_scope("sum_lines"):
        part = jnp.sum(part.reshape(4, 4, 2, 8, 2 * MY).astype(jnp.float32), 1)
        part = part.astype(jnp.bfloat16).reshape(8, 2, 4, 2 * MY).transpose(1, 0, 2, 3)
        part = jnp.broadcast_to(part[:, None], (2, 4, 8, 4, 2 * MY)).reshape(64, 4, 2 * MY)
    with jax.named_scope("gather_chan"):
        part = lax.all_to_all(part, ("yh", "yl", "core"), 0, 0, tiled=True)
        part, cross = lax.optimization_barrier((part, cross))
        zed = jnp.sum(part.reshape(2, 32, 4, 2 * MY).astype(jnp.float32), 0).astype(jnp.bfloat16)
    with jax.named_scope("mix"):
        zed_re = zed[..., :MY].astype(jnp.float32)
        zed_im = zed[..., MY:].astype(jnp.float32)
        wgt_re = spec_weight[0].astype(jnp.float32)
        wgt_im = spec_weight[1].astype(jnp.float32)
        mix_re = jnp.einsum("kiop,ikp->okp", wgt_re, zed_re) - jnp.einsum(
            "kiop,ikp->okp", wgt_im, zed_im
        )
        mix_im = jnp.einsum("kiop,ikp->okp", wgt_re, zed_im) + jnp.einsum(
            "kiop,ikp->okp", wgt_im, zed_re
        )
        mixed = jnp.concatenate([mix_re, mix_im], -1).astype(jnp.bfloat16)
    mixed, half = lax.optimization_barrier((mixed, half))
    with jax.named_scope("join_halves"):
        other = lax.ppermute(mixed, "yh", PAIR)
        other, following, end = lax.optimization_barrier((other, following, end))
        following, end = send(following), send(end)
        first = lax.axis_index("yh") == 0
        mixed = jnp.concatenate(
            [jnp.where(first, mixed, other), jnp.where(first, other, mixed)], 1
        )
        mixed = mixed.reshape(4, 1, 2, 8, 2 * MY)
        mixed = jnp.broadcast_to(mixed, (4, 4, 2, 8, 2 * MY)).reshape(32, 8, 2 * MY)
    with jax.named_scope("spread_modes"):
        modes = lax.all_to_all(mixed, column, 0, 0, tiled=True).reshape(MX, 2 * MY)
    with jax.named_scope("pointwise"):
        point = [pointwise(RAW_CUTS[j], image, sibling, cross[j], kron) for j in range(2)]
    modes, point[0], following = lax.optimization_barrier((modes, point[0], following))
    with jax.named_scope("rowback"):
        mode_re, mode_im = modes[:, :MY], modes[:, MY:]
        turned = jnp.concatenate([modes, jnp.concatenate([-mode_im, mode_re], 1)], 0)
        back = jnp.dot(row_tab, turned, preferred_element_type=jnp.float32)
        back = (back * (1.0 / math.sqrt(MX) / math.sqrt(MY))).astype(jnp.bfloat16)
        back = back.reshape(8, rows, 2 * MY)
    with jax.named_scope("swap_back"):
        back = lax.all_to_all(back, group, 0, 0, tiled=True)
    out = most(back, back_cols, bias_rows, *point, soon, following)
    back_tiles = jnp.asarray(np.ascontiguousarray(cols_np[-3 * TILE :].T))
    return rest(back, back_tiles, bias_rows, late, half, end, out)


def solution(mesh):
    fine = Mesh(mesh.devices.reshape(4, 2, 4, 2, 2, 2), ("x", "yh", "zh", "zl", "yl", "core"))
    row, chan = ("x", "yh", "zh", "zl"), ("yl", "core")
    in_specs = (P(chan, row, None), P(None, row, None, chan, None), P(), P(chan))
    return jax.shard_map(
        on_device, mesh=fine, in_specs=in_specs, out_specs=P(chan, row, None), check_vma=False
    )
```

```python
import functools
import math

import jax
import jax.numpy as jnp
import ml_dtypes
import numpy as np
from jax import lax
from jax.experimental import pallas as pl
from jax.experimental.pallas import tpu as pltpu
from jax.sharding import Mesh, PartitionSpec as P

H = 4096
W = 4096
MX = 256
MY = 256
PAIR = [(0, 1), (1, 0)]
GROUP = 16
VMEM = 56 * 2**20
SMALL = 16 * 2**20
TILE = 512
RAW = 2048
RAW_CUTS = (0, 1024, RAW)


def wave_table(points, freqs, length):
    prod = np.mod(points[:, None] * freqs[None, :], length)
    one = np.arange(length).astype(np.float32) * np.float32(2.0 * math.pi / length)
    return np.cos(one)[prod], np.sin(one)[prod]


def tables():
    cos_w, sin_w = wave_table(np.arange(W), np.arange(MY), W)
    cols = np.concatenate([cos_w, -sin_w], 1)
    freq = np.arange(MX).reshape(4, 2, 8, 4).transpose(0, 2, 1, 3).reshape(-1) - MX // 2
    cos_h, sin_h = wave_table(np.arange(H), freq, H)
    rows = np.concatenate([cos_h, sin_h], 1).reshape(4, 8, 2 * 64, 2 * MX)
    return cols.astype(ml_dtypes.bfloat16), rows.astype(ml_dtypes.bfloat16)


def spread(point_weight, outputs, inputs, chan):
    mine = lax.dynamic_slice(point_weight, (outputs * chan, 0), (chan, 4 * chan))
    order = jnp.concatenate(
        [lax.dynamic_slice(mine, (0, i * chan), (chan, chan)) for i in inputs], 1
    )
    n = len(inputs) * chan
    tall = np.kron(np.eye(chan), np.ones((GROUP, 1)))
    wide = np.kron(np.eye(n), np.ones((1, GROUP)))
    same = np.tile(np.eye(GROUP), (chan, n))
    full = jnp.dot(jnp.asarray(tall, jnp.bfloat16), order)
    full = jnp.dot(full, jnp.asarray(wide, jnp.bfloat16))
    return full * jnp.asarray(same, jnp.bfloat16)


def stack(refs, at):
    return jnp.concatenate([r[:, at, :].reshape(-1, TILE) for r in refs], 0)


def block(chan, rows, lo=0, hi=None):
    if hi is None:
        return pl.BlockSpec((chan, rows, TILE), lambda w: (0, 0, w + lo))
    return pl.BlockSpec(
        (chan, rows, TILE), lambda w: (0, 0, jnp.clip(w - lo, 0, hi - lo - 1))
    )


def product_kernel(
    own_ref, sib_ref, kron_ref, soon_ref, late_ref, half_ref, next_ref, end_ref
):
    step = pl.program_id(0)
    for t, (mine_ref, place, theirs) in enumerate(
        (
            (soon_ref, 0, ((next_ref, 0, 8),)),
            (late_ref, 0, ((half_ref, 0, 3), (end_ref, 0, 5))),
            (late_ref, 1, ((end_ref, 5, 8),)),
            (late_ref, 2, ((end_ref, 13, 8),)),
        )
    ):

        @pl.when(step == t)
        def _(mine_ref=mine_ref, place=place, theirs=theirs):
            for g in range(own_ref.shape[1] // GROUP):
                at = pl.ds(g * GROUP, GROUP)
                total = jnp.dot(
                    kron_ref[...],
                    stack((own_ref, sib_ref), at),
                    preferred_element_type=jnp.float32,
                )
                total = total.astype(jnp.bfloat16).reshape(16, GROUP, TILE)
                mine_ref[:, at, pl.ds(place * TILE, TILE)] = total[:8]
                done = 8
                for ref, lo, n in theirs:
                    ref[lo : lo + n, at, :] = total[done : done + n]
                    done += n


def product(image, sibling, kron):
    chan, rows, width = image.shape
    first, tiles = RAW // TILE, (width - RAW) // TILE
    sizes = [(chan, TILE), (chan, 3 * TILE), (3, TILE), (8, TILE), (21, TILE)]
    return pl.pallas_call(
        product_kernel,
        grid=(tiles,),
        in_specs=[block(chan, rows, first)] * 2 + [pl.BlockSpec(kron.shape, lambda w: (0, 0))],
        out_specs=[pl.BlockSpec((n, rows, w), lambda w: (0, 0, 0)) for n, w in sizes],
        out_shape=[jax.ShapeDtypeStruct((n, rows, w), jnp.bfloat16) for n, w in sizes],
        compiler_params=pltpu.CompilerParams(vmem_limit_bytes=VMEM),
        cost_estimate=pl.CostEstimate(
            flops=4 * 8 * rows * TILE * 256 * tiles,
            bytes_accessed=2**21 * tiles,
            transcendentals=0,
        ),
        name="product",
    )(image, sibling, kron)


def pointwise_kernel(own_ref, sib_ref, cross_ref, csib_ref, kron_ref, out_ref):
    for g in range(own_ref.shape[1] // GROUP):
        at = pl.ds(g * GROUP, GROUP)
        total = jnp.dot(
            kron_ref[...],
            stack((own_ref, sib_ref, cross_ref, csib_ref), at),
            preferred_element_type=jnp.float32,
        )
        out_ref[:, at, :] = total.astype(jnp.bfloat16).reshape(8, GROUP, TILE)


def pointwise(begin, image, sibling, cross, kron):
    chan, rows, width = cross.shape
    steps = width // TILE
    return pl.pallas_call(
        pointwise_kernel,
        grid=(steps,),
        in_specs=[block(chan, rows, begin // TILE)] * 2
        + [block(chan, rows)] * 2
        + [pl.BlockSpec(kron.shape, lambda w: (0, 0))],
        out_specs=block(chan, rows),
        out_shape=jax.ShapeDtypeStruct(cross.shape, jnp.bfloat16),
        compiler_params=pltpu.CompilerParams(vmem_limit_bytes=VMEM),
        cost_estimate=pl.CostEstimate(
            flops=2 * 8 * rows * width * 512,
            bytes_accessed=5 * 2**19 * steps,
            transcendentals=0,
        ),
        name="pointwise",
    )(image, sibling, cross, lax.ppermute(cross, "core", PAIR), kron)


def finish(rb_ref, back_ref, bias_ref, terms, out_ref, place=0):
    cols = pl.ds(place * TILE, TILE)
    for g in range(rb_ref.shape[1] // GROUP):
        at = pl.ds(g * GROUP, GROUP)
        total = jnp.dot(
            rb_ref[:, at, :].reshape(8 * GROUP, 2 * MY),
            back_ref[:, cols],
            preferred_element_type=jnp.float32,
        )
        for term in terms:
            term = [
                ref[lo : lo + n, at, pl.ds(c, TILE)].reshape(n * GROUP, TILE)
                for ref, lo, n, c in term
            ]
            total += jnp.concatenate(term, 0).astype(jnp.float32)
        total += bias_ref[...]
        out = 0.5 * total * (1.0 + lax.erf(total * math.sqrt(0.5)))
        out_ref[:, at, :] = out.astype(jnp.bfloat16).reshape(8, GROUP, TILE)


def most_kernel(rb_ref, back_ref, bias_ref, first_ref, second_ref, soon_ref, next_ref, out_ref):
    column = pl.program_id(0) * TILE

    @pl.when(column < RAW_CUTS[1])
    def _():
        finish(rb_ref, back_ref, bias_ref, ([(first_ref, 0, 8, 0)],), out_ref)

    @pl.when((column >= RAW_CUTS[1]) & (column < RAW))
    def _():
        finish(rb_ref, back_ref, bias_ref, ([(second_ref, 0, 8, 0)],), out_ref)

    @pl.when(column >= RAW)
    def _():
        terms = ([(soon_ref, 0, 8, 0)], [(next_ref, 0, 8, 0)])
        finish(rb_ref, back_ref, bias_ref, terms, out_ref)


def most(rb, back_cols, bias_rows, first, second, soon, following):
    chan, rows, _ = rb.shape
    width = back_cols.shape[1]
    cuts = [c // TILE for c in RAW_CUTS]

    def still(array):
        return pl.BlockSpec(array.shape, lambda w: (0,) * array.ndim)

    return pl.pallas_call(
        most_kernel,
        grid=(cuts[2] + 1,),
        in_specs=[
            pl.BlockSpec(memory_space=pltpu.VMEM),
            pl.BlockSpec((2 * MY, TILE), lambda w: (0, w)),
            still(bias_rows),
            block(chan, rows, 0, cuts[1]),
            block(chan, rows, cuts[1], cuts[2]),
            still(soon),
            still(following),
        ],
        out_specs=block(chan, rows),
        out_shape=jax.ShapeDtypeStruct((chan, rows, width), jnp.bfloat16),
        compiler_params=pltpu.CompilerParams(vmem_limit_bytes=56 * 2**20),
        cost_estimate=pl.CostEstimate(flops=1, bytes_accessed=1, transcendentals=0),
        name="most",
    )(rb, back_cols, bias_rows, first, second, soon, following)


def rest_kernel(rb_ref, back_ref, bias_ref, late_ref, half_ref, end_ref, so_far_ref, out_ref):
    others = (
        [(half_ref, 0, 3, 0), (end_ref, 0, 5, 0)],
        [(end_ref, 5, 8, 0)],
        [(end_ref, 13, 8, 0)],
    )
    for t, other in enumerate(others):

        @pl.when(pl.program_id(0) == t)
        def _(t=t, other=other):
            terms = ([(late_ref, 0, 8, t * TILE)], other)
            finish(rb_ref, back_ref, bias_ref, terms, out_ref, t)


def rest(rb, back_tiles, bias_rows, late, half, end, so_far):
    chan, rows, width = so_far.shape
    whole = pl.BlockSpec(memory_space=pltpu.VMEM)
    return pl.pallas_call(
        rest_kernel,
        grid=(3,),
        in_specs=[whole] * 6 + [pl.BlockSpec(memory_space=pl.ANY)],
        out_specs=block(chan, rows, width // TILE - 3),
        out_shape=jax.ShapeDtypeStruct(so_far.shape, jnp.bfloat16),
        input_output_aliases={6: 0},
        compiler_params=pltpu.CompilerParams(vmem_limit_bytes=SMALL),
        cost_estimate=pl.CostEstimate(flops=1, bytes_accessed=1, transcendentals=0),
        name="rest",
    )(rb, back_tiles, bias_rows, late, half, end, so_far)


def on_device(image, spec_weight, point_weight, bias):
    chan, rows, width = image.shape
    cols_np, rows_np = tables()
    fwd_cols = jnp.asarray(cols_np)
    back_cols = jnp.asarray(np.ascontiguousarray(cols_np.T))
    row_at = lax.axis_index(("yh", "zh"))
    row_tab = lax.dynamic_slice_in_dim(jnp.asarray(rows_np), row_at, 1, 1).reshape(
        8 * rows, 2 * MX
    )
    group, column = ("x", "zl"), ("x", "zh", "zl")

    def send(src):
        return lax.ppermute(src, "yl", PAIR)

    def raw(src, j):
        return src[:, :, RAW_CUTS[j] : RAW_CUTS[j + 1]]

    first, later = lax.optimization_barrier((raw(image, 0), image))
    cross = [send(first)]
    sibling = lax.ppermute(later, "core", PAIR)
    with jax.named_scope("point_weights"):
        me = lax.axis_index(("yl", "core"))
        kron = spread(point_weight, me, [me, me ^ 1, me ^ 2, me ^ 3], chan)
        kron_other = spread(point_weight, me ^ 2, [me, me ^ 1], chan)
        kron_both = jnp.concatenate([kron[:, : kron.shape[1] // 2], kron_other], 0)
        bias_rows = jnp.repeat(bias, GROUP)[:, None]

    with jax.named_scope("colspec"):
        colspec = jnp.dot(
            image.reshape(chan * rows, width), fwd_cols, preferred_element_type=jnp.float32
        )
        colspec = (colspec * (1.0 / math.sqrt(W))).astype(jnp.bfloat16)
    later, _ = lax.optimization_barrier((image, colspec))
    cross += [send(raw(later, j)) for j in range(1, len(RAW_CUTS) - 1)]
    with jax.named_scope("swap_rows"):
        line = lax.all_to_all(colspec.reshape(chan, rows, 2 * MY), group, 0, 0, tiled=True)
    line = line.reshape(8 * rows, 2 * MY)
    line, cross[0] = lax.optimization_barrier((line, cross[0]))
    with jax.named_scope("row_dft"):
        part = lax.dot_general(
            row_tab, line, (((0,), (0,)), ((), ())), preferred_element_type=jnp.float32
        )
        spec_re = part[:MX, :MY] + part[MX:, MY:]
        spec_im = part[:MX, MY:] - part[MX:, :MY]
        part = jnp.concatenate([spec_re, spec_im], -1) * (1.0 / math.sqrt(H))
        part = part.astype(jnp.bfloat16).reshape(32, 8, 2 * MY)
    with jax.named_scope("swap_modes"):
        part = lax.all_to_all(part, column, 0, 0, tiled=True)
    with jax.named_scope("products"):
        soon, late, half, following, end = product(image, sibling, kron_both)
    part, kron, bias_rows, soon, late, half, following, end = lax.optimization_barrier(
        (part, kron, bias_rows, soon, late, half, following, end)
    )
    half = send(half)
    with jax.named_scope("sum_lines"):
        part = jnp.sum(part.reshape(4, 4, 2, 8, 2 * MY).astype(jnp.float32), 1)
        part = part.astype(jnp.bfloat16).reshape(8, 2, 4, 2 * MY).transpose(1, 0, 2, 3)
        part = jnp.broadcast_to(part[:, None], (2, 4, 8, 4, 2 * MY)).reshape(64, 4, 2 * MY)
    with jax.named_scope("gather_chan"):
        part = lax.all_to_all(part, ("yh", "yl", "core"), 0, 0, tiled=True)
        part, cross = lax.optimization_barrier((part, cross))
        zed = jnp.sum(part.reshape(2, 32, 4, 2 * MY).astype(jnp.float32), 0).astype(jnp.bfloat16)
    with jax.named_scope("mix"):
        zed_re = zed[..., :MY].astype(jnp.float32)
        zed_im = zed[..., MY:].astype(jnp.float32)
        wgt_re = spec_weight[0].astype(jnp.float32)
        wgt_im = spec_weight[1].astype(jnp.float32)
        mix_re = jnp.einsum("kiop,ikp->okp", wgt_re, zed_re) - jnp.einsum(
            "kiop,ikp->okp", wgt_im, zed_im
        )
        mix_im = jnp.einsum("kiop,ikp->okp", wgt_re, zed_im) + jnp.einsum(
            "kiop,ikp->okp", wgt_im, zed_re
        )
        mixed = jnp.concatenate([mix_re, mix_im], -1).astype(jnp.bfloat16)
    mixed, half = lax.optimization_barrier((mixed, half))
    with jax.named_scope("join_halves"):
        other = lax.ppermute(mixed, "yh", PAIR)
        other, following, end = lax.optimization_barrier((other, following, end))
        following, end = send(following), send(end)
        first = lax.axis_index("yh") == 0
        mixed = jnp.concatenate(
            [jnp.where(first, mixed, other), jnp.where(first, other, mixed)], 1
        )
        mixed = mixed.reshape(4, 1, 2, 8, 2 * MY)
        mixed = jnp.broadcast_to(mixed, (4, 4, 2, 8, 2 * MY)).reshape(32, 8, 2 * MY)
    with jax.named_scope("spread_modes"):
        modes = lax.all_to_all(mixed, column, 0, 0, tiled=True).reshape(MX, 2 * MY)
    with jax.named_scope("pointwise"):
        point = [pointwise(RAW_CUTS[j], image, sibling, cross[j], kron) for j in range(2)]
    modes, point[0], following = lax.optimization_barrier((modes, point[0], following))
    with jax.named_scope("rowback"):
        mode_re, mode_im = modes[:, :MY], modes[:, MY:]
        turned = jnp.concatenate([modes, jnp.concatenate([-mode_im, mode_re], 1)], 0)
        back = jnp.dot(row_tab, turned, preferred_element_type=jnp.float32)
        back = (back * (1.0 / math.sqrt(MX) / math.sqrt(MY))).astype(jnp.bfloat16)
        back = back.reshape(8, rows, 2 * MY)
    with jax.named_scope("swap_back"):
        back = lax.all_to_all(back, group, 0, 0, tiled=True)
    out = most(back, back_cols, bias_rows, *point, soon, following)
    back_tiles = jnp.asarray(np.ascontiguousarray(cols_np[-3 * TILE :].T))
    return rest(back, back_tiles, bias_rows, late, half, end, out)


def solution(mesh):
    fine = Mesh(mesh.devices.reshape(4, 2, 4, 2, 2, 2), ("x", "yh", "zh", "zl", "yl", "core"))
    row, chan = ("x", "yh", "zh", "zl"), ("yl", "core")
    in_specs = (P(chan, row, None), P(None, row, None, chan, None), P(), P(chan))
    return jax.shard_map(
        on_device, mesh=fine, in_specs=in_specs, out_specs=P(chan, row, None), check_vma=False
    )
```
